32 devices in a mesh: frame: 4 (over y, x), crop: 4 (over z), dp: 2 (over core).
Axes of the slice: x: 2, y: 2, z: 4, core: 2. Of those that a mesh axis runs over, the one named last changes fastest.
Arguments:
- global_clips: bfloat16 [2, 16, 256, 1408], P('dp', 'frame', 'crop'), may hold values from -6 to 6
- frame_map: int32 [2, 16, 8], P('dp', 'crop'), may hold values from 0 to 15
- teacher_qkv: bfloat16 [1408, 4224], P(None, 'frame'), may hold values from -0.15625 to 0.15625
- teacher_out: bfloat16 [1408, 1408], P('frame'), may hold values from -0.15625 to 0.15625
- teacher_bottle: bfloat16 [1408, 256], replicated, may hold values from -0.15625 to 0.15625
- student_qkv: bfloat16 [1408, 4224], P(None, 'frame'), may hold values from -0.15625 to 0.15625
- student_out: bfloat16 [1408, 1408], P('frame'), may hold values from -0.15625 to 0.15625
- student_bottle: bfloat16 [1408, 256], replicated, may hold values from -0.15625 to 0.15625
- prototypes: bfloat16 [256, 8192], P(None, 'frame'), may hold values from -1.796875 to 1.796875
- center: float32 [8192], P('frame'), may hold values from -8.6 to -3.9
Outputs:
- grad_qkv: float32 [1408, 4224], P(('crop', 'dp'), 'frame')
- grad_out: float32 [1408, 1408], P('frame', ('crop', 'dp'))
- grad_bottle: float32 [1408, 256], P(('crop', 'dp'))
The draws below stay inside these ranges and needn't reach their ends.
All inputs are finite; a program needn't handle non-finite values.
Results may differ from the reference program's by a relative error of at most 0.00035.
Values may be sent and summed in bfloat16 or wider, within the bound.
A program may use at most 128 MiB of HBM per device.

```python
import math
import jax
import jax.numpy as jnp
from jax import lax

D = 1408
HEADS = 16
FRAMES = 16
PATCHES = 256
LFRAMES = 8
LOCAL_DEV = 4
BOTTLE = 256
LPATCH = 64
NTOK = 512
LOCAL_CLIPS = 16
BATCH = 2
PROTOS = 8192
N_CROP = 4


def draw_global_clips(key, part):
    first, second = jax.random.split(key, 2)
    offset = 0.8 * jax.random.normal(first, (BATCH, 1, 1, D), jnp.float32)
    values = offset + jax.random.normal(second, (BATCH, FRAMES, PATCHES, D), jnp.float32)
    return jnp.clip(values, -6.0, 6.0).astype(jnp.bfloat16)


def draw_center(key, part):
    first = jax.random.fold_in(key, 7)
    noise = jnp.clip(0.1 * jax.random.normal(first, (PROTOS,), jnp.float32), -0.3, 0.3)
    values = -4.5 + noise
    return values.astype(jnp.float32)


def plant(values, stream_key, least, high):
    index_at = [jax.random.randint(jax.random.fold_in(stream_key, axis), (), 0, length) for axis, length in enumerate(values.shape)]
    widest = values.shape.index(max(values.shape))
    next_to = index_at[:widest] + [(index_at[widest] + 1) % values.shape[widest]] + index_at[widest + 1:]
    return values.at[tuple(index_at)].set(least).at[tuple(next_to)].set(high)


def shard_levels(rng, extent, cuts, low, top_value):
    factor_of, own = 1.0, jax.random.fold_in(rng, 6)
    for position, blocks in cuts:
        draws = jnp.exp(jax.random.uniform(jax.random.fold_in(own, position), (blocks,), jnp.float32, low / len(cuts), top_value / len(cuts)))
        factor_of = factor_of * jnp.repeat(draws, extent[position] // blocks).reshape([-1 if axis == position else 1 for axis in range(len(extent))])
    return factor_of


def normal_values(rng, shape, width, limit, pieces=(), held_as=jnp.bfloat16):
    entries = width * jax.random.normal(rng, shape, jnp.float32)
    if pieces:
        entries = entries * shard_levels(rng, shape, pieces, -0.22, 0.18)
    return jnp.clip(entries, -limit, limit).astype(held_as)


def setup_inputs(seed: int = 0) -> dict:
    splits = jax.random.split(jax.random.key(seed), 11)
    return {
        "global_clips": draw_global_clips(jax.random.fold_in(splits[10], 71), 0),
        "frame_map": plant(jax.random.randint(splits[1], (BATCH, LOCAL_CLIPS, LFRAMES), 0, FRAMES), jax.random.fold_in(splits[1], 1), 0, FRAMES - 1).astype(jnp.int32),
        "teacher_qkv": normal_values(splits[2], (D, 3 * D), D ** -0.5, 0.15625, ((1, 4),)),
        "teacher_out": normal_values(splits[3], (D, D), D ** -0.5, 0.15625, ((0, 4),)),
        "teacher_bottle": normal_values(splits[4], (D, BOTTLE), D ** -0.5, 0.15625),
        "student_qkv": normal_values(splits[5], (D, 3 * D), D ** -0.5, 0.15625, ((1, 4),)),
        "student_out": normal_values(splits[6], (D, D), D ** -0.5, 0.15625, ((0, 4),)),
        "student_bottle": normal_values(splits[7], (D, BOTTLE), D ** -0.5, 0.15625),
        "prototypes": normal_values(splits[8], (BOTTLE, PROTOS), 0.3, 1.796875, ((1, 4),)),
        "center": draw_center(jax.random.fold_in(splits[10], 71), 0),
    }


HIGH = lax.Precision.HIGHEST
TAU_TEACH = 0.04
TAU_STUD = 0.1

def norm_tokens(tokens):
    values = tokens.astype(jnp.float32)
    middle = lax.optimization_barrier(jnp.mean(values, axis=-1, keepdims=True))
    spread = lax.optimization_barrier(jnp.mean(jnp.square(values - middle), axis=-1, keepdims=True))
    return ((values - middle) * lax.rsqrt(spread + 1e-06)).astype(jnp.bfloat16)

def attend_core(qkv):
    rounded = lax.optimization_barrier(qkv.astype(jnp.bfloat16)).astype(jnp.float32)
    query = rounded[:, :, :, 0]
    keys = rounded[:, :, :, 1]
    values = rounded[:, :, :, 2]
    scale = 1.0 / math.sqrt(qkv.shape[-1])
    scores = jnp.einsum('iphe,jphe->phij', query, keys, precision=HIGH) * scale
    weights = jax.nn.softmax(scores, axis=-1)
    weights = lax.optimization_barrier(weights.astype(jnp.bfloat16)).astype(jnp.float32)
    return jnp.einsum('phij,jphe->iphe', weights, values, precision=HIGH)

def project(normed, weight32):
    qkv = jnp.einsum('fpd,dc->fpc', normed.astype(jnp.float32), weight32, precision=HIGH)
    return qkv.reshape(normed.shape[0], normed.shape[1], HEADS, 3, -1)

def unit(vector):
    return vector * lax.rsqrt(lax.optimization_barrier(jnp.sum(vector * vector, axis=-1, keepdims=True)) + 1e-06)

def reference(global_clips, frame_map, teacher_qkv, teacher_out, teacher_bottle, student_qkv, student_out, student_bottle, prototypes, center):
    protos = prototypes.astype(jnp.float32)
    t_qkv = teacher_qkv.astype(jnp.float32)
    t_out = teacher_out.astype(jnp.float32)
    t_bottle = teacher_bottle.astype(jnp.float32)
    s_qkv = student_qkv.astype(jnp.float32)
    s_out = student_out.astype(jnp.float32)
    s_bottle = student_bottle.astype(jnp.float32)
    crop_of = jnp.arange(LOCAL_CLIPS, dtype=jnp.int32) // LOCAL_DEV

    def one_clip(index):
        clip = lax.dynamic_index_in_dim(global_clips, index, 0, keepdims=False)
        maps = lax.dynamic_index_in_dim(frame_map, index, 0, keepdims=False)
        normed = norm_tokens(clip)
        t_att = attend_core(project(normed, t_qkv))
        t_mean = lax.optimization_barrier(jnp.sum(t_att, axis=(0, 1))).reshape(-1) / (FRAMES * PATCHES)
        pooled_t = lax.optimization_barrier(jnp.mean(clip.astype(jnp.float32), axis=(0, 1))) + jnp.dot(t_mean, t_out, precision=HIGH)
        unit_t = unit(jnp.dot(pooled_t, t_bottle, precision=HIGH))
        probs = jax.nn.softmax((jnp.dot(unit_t, protos, precision=HIGH) - center) / TAU_TEACH)
        crops = clip.reshape(FRAMES, N_CROP, LPATCH, D)
        local = crops[maps.T, crop_of[None, :]]
        local_mean = lax.optimization_barrier(jnp.mean(local.astype(jnp.float32), axis=(0, 2)))
        local_normed = norm_tokens(local).reshape(LFRAMES, LOCAL_CLIPS * LPATCH, D)

        def loss_fn(w_qkv, w_out, w_bottle):
            s_att = attend_core(project(local_normed, w_qkv))
            s_mean = lax.optimization_barrier(jnp.sum(s_att.reshape(LFRAMES, LOCAL_CLIPS, LPATCH, D), axis=(0, 2))) / NTOK
            pooled_s = local_mean + jnp.dot(s_mean, w_out, precision=HIGH)
            unit_s = unit(jnp.dot(pooled_s, w_bottle, precision=HIGH))
            log_q = jax.nn.log_softmax(jnp.dot(unit_s, protos, precision=HIGH) / TAU_STUD, axis=-1)
            return -jnp.sum(log_q * probs[None, :]) / LOCAL_CLIPS
        return jax.grad(loss_fn, argnums=(0, 1, 2))(s_qkv, s_out, s_bottle)
    grads = lax.map(one_clip, jnp.arange(BATCH, dtype=jnp.int32))
    return (lax.optimization_barrier(jnp.sum(grads[0], axis=0)), lax.optimization_barrier(jnp.sum(grads[1], axis=0)), lax.optimization_barrier(jnp.sum(grads[2], axis=0)))
```

```python
import functools
import math

import jax
import jax.numpy as jnp
from jax import lax
from jax.experimental import pallas as pl
from jax.experimental.pallas import tpu as pltpu
from jax.sharding import PartitionSpec as P

HEAD = 88
HIGH = lax.Precision.HIGHEST
TAU_TEACH = 0.04
TAU_STUD = 0.1
SCALE = 1.0 / math.sqrt(HEAD)
NT = (((1,), (1,)), ((), ()))


def rounded(x):
    return x.astype(jnp.bfloat16).astype(jnp.float32)


def forward_kernel(
    maps, tokens, w_t, w_s, normed, sums, t_heads, s_heads, s_qkv, s_weights, s_cols, picked, t_qkv
):
    frames = tokens.shape[0]
    half = tokens.shape[1]
    heads = w_t.shape[0] // (3 * HEAD)
    pairs = frames // 2
    clips, steps = maps.shape

    def norm(f, _):
        x = tokens[f].astype(jnp.float32)
        middle = jnp.mean(x, axis=-1, keepdims=True)
        away = x - middle
        spread = jnp.mean(away * away, axis=-1, keepdims=True)
        normed[f] = (away * lax.rsqrt(spread + 1e-06)).astype(jnp.bfloat16)
        sums[pl.ds(f, 1)] = jnp.sum(x, axis=0, keepdims=True)
        return 0

    lax.fori_loop(0, frames, norm, 0)

    def project_t(a, _):
        x = jnp.concatenate([normed[2 * a], normed[2 * a + 1]], axis=0)
        t_qkv[a] = rounded(
            lax.dot_general(w_t[...], x, NT, preferred_element_type=jnp.float32)
        )
        return 0

    lax.fori_loop(0, pairs, project_t, 0)

    def attend_t(h, _):
        row = pl.multiple_of(h * (3 * HEAD), 8)
        keys = t_qkv[:, pl.ds(row + HEAD, HEAD), :]
        turned = pltpu.roll(keys, half, 2)
        same = jnp.zeros((pairs, 2 * half), jnp.float32)
        cross = jnp.zeros((pairs, 2 * half), jnp.float32)
        for a in range(pairs):
            query = t_qkv[a, pl.ds(row, HEAD), :]
            one = jnp.sum(query[None] * keys, axis=1) * SCALE
            two = jnp.sum(query[None] * turned, axis=1) * SCALE
            top = jnp.maximum(
                jnp.max(one, axis=0, keepdims=True), jnp.max(two, axis=0, keepdims=True)
            )
            one = jnp.exp(one - top)
            two = jnp.exp(two - top)
            total = jnp.sum(one, axis=0, keepdims=True) + jnp.sum(two, axis=0, keepdims=True)
            same = same + rounded(one / total)
            cross = cross + rounded(two / total)
        columns = same + pltpu.roll(cross, half, 1)
        out = jnp.zeros((HEAD, 2 * half), jnp.float32)
        for b in range(pairs):
            out = out + columns[b : b + 1, :] * t_qkv[b, pl.ds(row + 2 * HEAD, HEAD), :]
        t_heads[pl.ds(pl.multiple_of(h * HEAD, 8), HEAD), :] = out
        return 0

    lax.fori_loop(0, heads, attend_t, 0)

    for lp in range(clips // 2):

        def project_s(i, _):
            x = jnp.concatenate([normed[maps[2 * lp, i]], normed[maps[2 * lp + 1, i]]], axis=0)
            picked[lp, i] = x
            s_qkv[lp, i] = rounded(
                lax.dot_general(w_s[...], x, NT, preferred_element_type=jnp.float32)
            )
            return 0

        lax.fori_loop(0, steps, project_s, 0)

        def attend_s(h, _):
            row = pl.multiple_of(h * (3 * HEAD), 8)
            keys = s_qkv[lp, :, pl.ds(row + HEAD, HEAD), :]
            columns = jnp.zeros((steps, 2 * half), jnp.float32)
            for i in range(steps):
                query = s_qkv[lp, i, pl.ds(row, HEAD), :]
                one = jnp.sum(query[None] * keys, axis=1) * SCALE
                one = jnp.exp(one - jnp.max(one, axis=0, keepdims=True))
                one = one / jnp.sum(one, axis=0, keepdims=True)
                s_weights[lp, h, i] = one
                columns = columns + rounded(one)
            s_cols[lp, h] = columns
            out = jnp.zeros((HEAD, 2 * half), jnp.float32)
            for j in range(steps):
                out = out + columns[j : j + 1, :] * s_qkv[lp, j, pl.ds(row + 2 * HEAD, HEAD), :]
            s_heads[lp, pl.ds(pl.multiple_of(h * HEAD, 8), HEAD), :] = out
            return 0

        lax.fori_loop(0, heads, attend_s, 0)


def backward_kernel(grads, s_qkv, s_weights, s_cols, picked, g_qkv, d_rows, d_all, x_turned):
    pairs, steps, width, lanes = s_qkv.shape
    heads = width // (3 * HEAD)

    for lp in range(pairs):

        def attend(h, _):
            row = pl.multiple_of(h * (3 * HEAD), 8)
            grad = grads[lp, pl.ds(pl.multiple_of(h * HEAD, 8), HEAD), :]
            values = s_qkv[lp, :, pl.ds(row + 2 * HEAD, HEAD), :]
            d_weights = rounded(jnp.sum(values * grad[None], axis=1))
            d_scores = []
            for i in range(steps):
                weights = s_weights[lp, h, i]
                inner = jnp.sum(weights * d_weights, axis=0, keepdims=True)
                d_scores.append(weights * (d_weights - inner) * SCALE)
            for i in range(steps):
                d_query = jnp.zeros((HEAD, lanes), jnp.float32)
                for j in range(steps):
                    d_query = (
                        d_query
                        + d_scores[i][j : j + 1, :] * s_qkv[lp, j, pl.ds(row + HEAD, HEAD), :]
                    )
                d_rows[i, pl.ds(row, HEAD), :] = d_query
            columns = s_cols[lp, h]
            for j in range(steps):
                d_key = jnp.zeros((HEAD, lanes), jnp.float32)
                for i in range(steps):
                    d_key = (
                        d_key + d_scores[i][j : j + 1, :] * s_qkv[lp, i, pl.ds(row, HEAD), :]
                    )
                d_rows[j, pl.ds(row + HEAD, HEAD), :] = d_key
                d_rows[j, pl.ds(row + 2 * HEAD, HEAD), :] = columns[j : j + 1, :] * grad
            return 0

        lax.fori_loop(0, heads, attend, 0)
        for i in range(steps):
            at = (lp * steps + i) * lanes
            d_all[:, at : at + lanes] = d_rows[i].astype(jnp.bfloat16)
            x_turned[:, at : at + lanes] = picked[lp, i].T

    depth = x_turned.shape[0]
    block = depth // 4

    def multiply(n, _):
        at = pl.multiple_of(n * block, 16)
        g_qkv[pl.ds(at, block), :] = lax.dot_general(
            x_turned[pl.ds(at, block), :], d_all[...], NT, preferred_element_type=jnp.float32
        )
        return 0

    lax.fori_loop(0, 4, multiply, 0)


def vmem(count):
    return [pl.BlockSpec(memory_space=pltpu.VMEM)] * count


def forward(maps, tokens, w_t, w_s):
    frames, patches, width = tokens.shape
    columns = w_t.shape[0]
    heads = columns // (3 * HEAD)
    clips, steps = maps.shape
    lanes = 2 * patches
    f32, bf16 = jnp.float32, jnp.bfloat16
    shape = jax.ShapeDtypeStruct
    return pl.pallas_call(
        forward_kernel,
        out_shape=[
            shape((frames, patches, width), bf16),
            shape((frames, width), f32),
            shape((heads * HEAD, lanes), f32),
            shape((clips // 2, heads * HEAD, lanes), f32),
            shape((clips // 2, steps, columns, lanes), f32),
            shape((clips // 2, heads, steps, steps, lanes), f32),
            shape((clips // 2, heads, steps, lanes), f32),
            shape((clips // 2, steps, lanes, width), bf16),
        ],
        in_specs=[pl.BlockSpec(memory_space=pltpu.SMEM)] + vmem(3),
        out_specs=vmem(8),
        scratch_shapes=[pltpu.VMEM((frames // 2, columns, lanes), f32)],
        compiler_params=pltpu.CompilerParams(vmem_limit_bytes=56 * 1024 * 1024),
    )(maps, tokens, w_t, w_s)


def backward(grads, s_qkv, s_weights, s_cols, picked):
    pairs, steps, columns, lanes = s_qkv.shape
    width = picked.shape[-1]
    return pl.pallas_call(
        backward_kernel,
        out_shape=jax.ShapeDtypeStruct((width, columns), jnp.float32),
        in_specs=vmem(5),
        out_specs=vmem(1)[0],
        scratch_shapes=[
            pltpu.VMEM((steps, columns, lanes), jnp.float32),
            pltpu.VMEM((columns, pairs * steps * lanes), jnp.bfloat16),
            pltpu.VMEM((width, pairs * steps * lanes), jnp.bfloat16),
        ],
        compiler_params=pltpu.CompilerParams(vmem_limit_bytes=56 * 1024 * 1024),
    )(grads, s_qkv, s_weights, s_cols, picked)


def unit(vector):
    return vector * lax.rsqrt(jnp.sum(vector * vector, axis=-1, keepdims=True) + 1e-06)


def local(
    global_clips,
    frame_map,
    teacher_qkv,
    teacher_out,
    teacher_bottle,
    student_qkv,
    student_out,
    student_bottle,
    prototypes,
    center,
):
    f32 = jnp.float32
    tokens = global_clips[0]
    maps = frame_map[0]
    gathered = lax.all_gather(tokens, "frame", axis=0, tiled=True)
    frames_all, patches, width = gathered.shape
    clips, steps = maps.shape
    spread = lax.axis_size("crop") * lax.axis_size("dp")
    place = lax.axis_index("crop") * lax.axis_size("dp") + lax.axis_index("dp")
    teacher_count = frames_all * patches * lax.axis_size("crop")
    local_count = steps * patches

    _, sums, t_wide, s_wide, s_qkv, s_weights, s_cols, picked = forward(
        maps, gathered, teacher_qkv.T, student_qkv.T
    )
    rows = t_wide.shape[0]
    t_heads = jnp.sum(t_wide, axis=1)
    s_heads = (
        jnp.sum(s_wide.reshape(clips // 2, rows, 2, patches), axis=3)
        .transpose(0, 2, 1)
        .reshape(clips, rows)
    ) / local_count

    t_out32 = teacher_out.astype(f32)
    s_out32 = student_out.astype(f32)
    s_bottle32 = student_bottle.astype(f32)
    protos = prototypes.astype(f32)
    own = jnp.sum(tokens, axis=(0, 1), dtype=f32)
    t_partial = (own + jnp.dot(t_heads, t_out32, precision=HIGH)) / teacher_count
    t_z = jnp.dot(t_partial, teacher_bottle.astype(f32), precision=HIGH)
    s_partial = jnp.dot(s_heads, s_out32, precision=HIGH)
    picks = jnp.sum(
        (maps[:, :, None] == jnp.arange(frames_all, dtype=jnp.int32)[None, None, :]).astype(f32),
        axis=1,
    )
    local_mean = jnp.dot(picks, sums, precision=HIGH) / local_count

    packed = lax.psum(jnp.concatenate([s_partial.reshape(-1), t_z]), "frame")
    s_pooled = local_mean + packed[: clips * width].reshape(clips, width)
    unit_t = unit(lax.psum(packed[clips * width :], "crop"))
    s_z = jnp.dot(s_pooled, s_bottle32, precision=HIGH)
    inverse = lax.rsqrt(jnp.sum(s_z * s_z, axis=-1, keepdims=True) + 1e-06)
    unit_s = s_z * inverse

    units = jnp.concatenate([unit_s, unit_t[None]], axis=0)
    raw = jnp.dot(units, protos, precision=HIGH)
    logits = jnp.concatenate([raw[:clips] / TAU_STUD, (raw[clips:] - center) / TAU_TEACH], axis=0)
    top = jnp.max(logits, axis=-1, keepdims=True)
    weights = jnp.exp(logits - top)
    total = jnp.sum(weights, axis=-1, keepdims=True)
    expect = lax.dot_general(weights, protos, NT, precision=HIGH)
    shares = lax.all_gather(jnp.concatenate([expect, total, top], axis=1), "frame")
    bottle = expect.shape[1]
    tops = shares[:, :, bottle + 1 :]
    factor = jnp.exp(tops - jnp.max(tops, axis=0, keepdims=True))
    merged = jnp.sum(shares[:, :, : bottle + 1] * factor, axis=0)
    expect = merged[:, :bottle] / merged[:, bottle:]

    all_clips = clips * lax.axis_size("crop")
    d_unit = (expect[:clips] - expect[clips:]) / (all_clips * TAU_STUD)
    d_z = (d_unit - unit_s * jnp.sum(unit_s * d_unit, axis=-1, keepdims=True)) * inverse
    d_pooled = lax.dot_general(d_z, s_bottle32, NT, precision=HIGH)
    d_heads = lax.dot_general(d_pooled, s_out32, NT, precision=HIGH) / local_count

    wide = jnp.broadcast_to(
        d_heads.reshape(clips // 2, 2, rows).transpose(0, 2, 1)[..., None],
        (clips // 2, rows, 2, patches),
    ).reshape(clips // 2, rows, 2 * patches)
    g_qkv = backward(wide, s_qkv, s_weights, s_cols, picked)
    g_qkv = lax.psum_scatter(g_qkv, ("crop", "dp"), scatter_dimension=0, tiled=True)

    few = lax.all_gather(
        jnp.concatenate([s_heads, s_pooled, d_z], axis=1), ("crop", "dp"), axis=0, tiled=True
    )
    size = width // spread
    all_heads = few[:, :rows]
    all_pooled = lax.dynamic_slice_in_dim(few[:, rows : rows + width], place * size, size, axis=1)
    all_d_z = few[:, rows + width :]
    some_bottle = lax.dynamic_slice_in_dim(s_bottle32, place * size, size, axis=0)
    g_bottle = jnp.dot(all_pooled.T, all_d_z, precision=HIGH)
    d_some = lax.dot_general(all_d_z, some_bottle, NT, precision=HIGH)
    g_out = jnp.dot(all_heads.T, d_some, precision=HIGH)
    return g_qkv, g_out, g_bottle


def solution(mesh):
    return jax.shard_map(
        local,
        mesh=mesh,
        in_specs=(
            P("dp", "frame", "crop", None),
            P("dp", "crop", None),
            P(None, "frame"),
            P("frame", None),
            P(),
            P(None, "frame"),
            P("frame", None),
            P(),
            P(None, "frame"),
            P("frame"),
        ),
        out_specs=(P(("crop", "dp"), "frame"), P("frame", ("crop", "dp")), P(("crop", "dp"), None)),
        check_vma=False,
    )
```

```python
import functools
import math

import jax
import jax.numpy as jnp
from jax import lax
from jax.experimental import pallas as pl
from jax.experimental.pallas import tpu as pltpu
from jax.sharding import PartitionSpec as P

HEAD = 88
HIGH = lax.Precision.HIGHEST
TAU_TEACH = 0.04
TAU_STUD = 0.1
SCALE = 1.0 / math.sqrt(HEAD)
NT = (((1,), (1,)), ((), ()))


def rounded(x):
    return x.astype(jnp.bfloat16).astype(jnp.float32)


MESH = pl.DeviceIdType.MESH


def greet(peers):
    barrier = pltpu.get_barrier_semaphore()
    for peer in peers:
        pl.semaphore_signal(barrier, inc=1, device_id=peer, device_id_type=MESH)
    pl.semaphore_wait(barrier, len(peers))


def gather_kernel(
    count, tokens, w_t, w_s, normed, sums, t_qkv, s_frames, held, send_sems, recv_sems
):
    me = lax.axis_index("frame")
    each = tokens.shape[0]
    half = tokens.shape[1]
    peers = [{"frame": lax.rem(me + s, count)} for s in range(1, count)]
    greet(peers)
    copies = []
    for s, peer in enumerate(peers):
        copy = pltpu.make_async_remote_copy(
            src_ref=tokens,
            dst_ref=held.at[me],
            send_sem=send_sems.at[s],
            recv_sem=recv_sems.at[s],
            device_id=peer,
            device_id_type=MESH,
        )
        copy.start()
        copies.append(copy)

    def norm(x, f):
        x = x.astype(jnp.float32)
        middle = jnp.mean(x, axis=-1, keepdims=True)
        away = x - middle
        spread = jnp.mean(away * away, axis=-1, keepdims=True)
        out = (away * lax.rsqrt(spread + 1e-06)).astype(jnp.bfloat16)
        normed[f] = out
        sums[f] = jnp.sum(x, axis=0, keepdims=True)

    def project(pair):
        f = 2 * pair
        x = jnp.concatenate([normed[f], normed[f + 1]], axis=0)
        t_qkv[pair] = lax.dot_general(
            w_t[...], x, NT, preferred_element_type=jnp.float32
        ).astype(jnp.bfloat16)
        y = lax.dot_general(w_s[...], x, NT, preferred_element_type=jnp.float32)
        turned = pltpu.roll(y, half, 1)
        low = lax.broadcasted_iota(jnp.int32, y.shape, 1) < half
        s_frames[f] = jnp.where(low, y, turned).astype(jnp.bfloat16)
        s_frames[f + 1] = jnp.where(low, turned, y).astype(jnp.bfloat16)

    paired = each % 2 == 0

    def work(load, source):
        def one(k, _):
            norm(load(k), source * each + k)
            return 0

        def two(k, _):
            project(source * (each // 2) + k)
            return 0

        lax.fori_loop(0, each, one, 0)
        if paired:
            lax.fori_loop(0, each // 2, two, 0)

    work(lambda k: tokens[k], me)
    for s in range(1, count):
        copies[s - 1].wait_recv()
        source = lax.rem(me + count - s, count)
        work(lambda k, source=source: held[source, k], source)
    if not paired:

        def late(k, _):
            project(k)
            return 0

        lax.fori_loop(0, t_qkv.shape[0], late, 0)
    for copy in copies:
        copy.wait_send()


def share_sum_kernel(
    frames, crops, part, small, part_sum, small_sum, held, held_small, sends, recvs, sends_b, recvs_b
):
    me = lax.axis_index("frame")
    layer = lax.axis_index("crop")
    mine = layer * frames + me
    shifts = [(c, s) for c in range(crops) for s in range(frames) if c + s > 0]
    peers = [
        {"frame": lax.rem(me + s, frames), "crop": lax.rem(layer + c, crops)} for c, s in shifts
    ]
    greet(peers)
    copies = []
    for n, ((c, s), peer) in enumerate(zip(shifts, peers)):
        if c == 0:
            copies.append(
                pltpu.make_async_remote_copy(
                    src_ref=part,
                    dst_ref=held.at[me],
                    send_sem=sends.at[s - 1],
                    recv_sem=recvs.at[s - 1],
                    device_id=peer,
                    device_id_type=MESH,
                )
            )
            copies[-1].start()
    for n, peer in enumerate(peers):
        copies.append(
            pltpu.make_async_remote_copy(
                src_ref=small,
                dst_ref=held_small.at[mine],
                send_sem=sends_b.at[n],
                recv_sem=recvs_b.at[n],
                device_id=peer,
                device_id_type=MESH,
            )
        )
        copies[-1].start()
    held[me] = part[...]
    held_small[mine] = small[...]
    for copy in copies:
        copy.wait()
    total = held[0]
    for f in range(1, frames):
        total = total + held[f]
    part_sum[...] = total
    total = held_small[0]
    for f in range(1, frames * crops):
        total = total + held_small[f]
    small_sum[...] = total


def share_kernel(frames, part, out, held, sends, recvs):
    me = lax.axis_index("frame")
    peers = [{"frame": lax.rem(me + s, frames)} for s in range(1, frames)]
    greet(peers)
    copies = []
    for n, peer in enumerate(peers):
        copies.append(
            pltpu.make_async_remote_copy(
                src_ref=part,
                dst_ref=held.at[me],
                send_sem=sends.at[n],
                recv_sem=recvs.at[n],
                device_id=peer,
                device_id_type=MESH,
            )
        )
        copies[-1].start()
    held[me] = part[...]
    for copy in copies:
        copy.wait()
    out[...] = held[...]


def forward_kernel(
    maps, t_half, s_frames, t_heads, s_heads, s_qkv, s_weights, s_cols, t_qkv
):
    pairs, columns_all, lanes = t_half.shape
    half = lanes // 2
    heads = columns_all // (3 * HEAD)
    clips, steps = maps.shape

    def widen(a, _):
        t_qkv[a] = t_half[a].astype(jnp.float32)
        return 0

    lax.fori_loop(0, pairs, widen, 0)

    def attend_t(h, _):
        row = pl.multiple_of(h * (3 * HEAD), 8)
        keys = t_qkv[:, pl.ds(row + HEAD, HEAD), :]
        turned = pltpu.roll(keys, half, 2)
        same = jnp.zeros((pairs, 2 * half), jnp.float32)
        cross = jnp.zeros((pairs, 2 * half), jnp.float32)
        for a in range(pairs):
            query = t_qkv[a, pl.ds(row, HEAD), :]
            one = jnp.sum(query[None] * keys, axis=1) * SCALE
            two = jnp.sum(query[None] * turned, axis=1) * SCALE
            top = jnp.maximum(
                jnp.max(one, axis=0, keepdims=True), jnp.max(two, axis=0, keepdims=True)
            )
            one = jnp.exp(one - top)
            two = jnp.exp(two - top)
            total = jnp.sum(one, axis=0, keepdims=True) + jnp.sum(two, axis=0, keepdims=True)
            same = same + rounded(one / total)
            cross = cross + rounded(two / total)
        columns = same + pltpu.roll(cross, half, 1)
        out = jnp.zeros((HEAD, 2 * half), jnp.float32)
        for b in range(pairs):
            out = out + columns[b : b + 1, :] * t_qkv[b, pl.ds(row + 2 * HEAD, HEAD), :]
        t_heads[pl.ds(pl.multiple_of(h * HEAD, 8), HEAD), :] = out
        return 0

    lax.fori_loop(0, heads, attend_t, 0)

    for lp in range(clips // 2):

        def project_s(i, _):
            low = lax.broadcasted_iota(jnp.int32, (columns_all, lanes), 1) < half
            s_qkv[lp, i] = jnp.where(
                low,
                s_frames[maps[2 * lp, i]].astype(jnp.float32),
                s_frames[maps[2 * lp + 1, i]].astype(jnp.float32),
            )
            return 0

        lax.fori_loop(0, steps, project_s, 0)

        def attend_s(h, _):
            row = pl.multiple_of(h * (3 * HEAD), 8)
            keys = s_qkv[lp, :, pl.ds(row + HEAD, HEAD), :]
            columns = jnp.zeros((steps, 2 * half), jnp.float32)
            for i in range(steps):
                query = s_qkv[lp, i, pl.ds(row, HEAD), :]
                one = jnp.sum(query[None] * keys, axis=1) * SCALE
                one = jnp.exp(one - jnp.max(one, axis=0, keepdims=True))
                one = one / jnp.sum(one, axis=0, keepdims=True)
                s_weights[lp, h, i] = one
                columns = columns + rounded(one)
            s_cols[lp, h] = columns
            out = jnp.zeros((HEAD, 2 * half), jnp.float32)
            for j in range(steps):
                out = out + columns[j : j + 1, :] * s_qkv[lp, j, pl.ds(row + 2 * HEAD, HEAD), :]
            s_heads[lp, pl.ds(pl.multiple_of(h * HEAD, 8), HEAD), :] = out
            return 0

        lax.fori_loop(0, heads, attend_s, 0)


def backward_kernel(
    first, heads, maps, grads, s_qkv, s_weights, s_cols, normed, g_qkv, d_rows, d_all, x_turned
):
    pairs, steps, _, lanes = s_qkv.shape

    for lp in range(pairs):

        def attend(n, _):
            h = first + n
            row = pl.multiple_of(h * (3 * HEAD), 8)
            own = pl.multiple_of(n * (3 * HEAD), 8)
            grad = grads[lp, pl.ds(pl.multiple_of(h * HEAD, 8), HEAD), :]
            values = s_qkv[lp, :, pl.ds(row + 2 * HEAD, HEAD), :]
            d_weights = rounded(jnp.sum(values * grad[None], axis=1))
            d_scores = []
            for i in range(steps):
                weights = s_weights[lp, h, i]
                inner = jnp.sum(weights * d_weights, axis=0, keepdims=True)
                d_scores.append(weights * (d_weights - inner) * SCALE)
            for i in range(steps):
                d_query = jnp.zeros((HEAD, lanes), jnp.float32)
                for j in range(steps):
                    d_query = (
                        d_query
                        + d_scores[i][j : j + 1, :] * s_qkv[lp, j, pl.ds(row + HEAD, HEAD), :]
                    )
                d_rows[i, pl.ds(own, HEAD), :] = d_query
            columns = s_cols[lp, h]
            for j in range(steps):
                d_key = jnp.zeros((HEAD, lanes), jnp.float32)
                for i in range(steps):
                    d_key = (
                        d_key + d_scores[i][j : j + 1, :] * s_qkv[lp, i, pl.ds(row, HEAD), :]
                    )
                d_rows[j, pl.ds(own + HEAD, HEAD), :] = d_key
                d_rows[j, pl.ds(own + 2 * HEAD, HEAD), :] = columns[j : j + 1, :] * grad
            return 0

        lax.fori_loop(0, heads, attend, 0)
        for i in range(steps):
            at = (lp * steps + i) * lanes
            d_all[:, at : at + lanes] = d_rows[i].astype(jnp.bfloat16)
            x = jnp.concatenate([normed[maps[2 * lp, i]], normed[maps[2 * lp + 1, i]]], axis=0)
            x_turned[:, at : at + lanes] = x.T

    depth = x_turned.shape[0]
    block = depth // 4

    def multiply(n, _):
        at = pl.multiple_of(n * block, 16)
        g_qkv[pl.ds(at, block), :] = lax.dot_general(
            x_turned[pl.ds(at, block), :], d_all[...], NT, preferred_element_type=jnp.float32
        )
        return 0

    lax.fori_loop(0, 4, multiply, 0)


def vmem(count):
    return [pl.BlockSpec(memory_space=pltpu.VMEM)] * count


def limits(**more):
    return pltpu.CompilerParams(vmem_limit_bytes=56 * 1024 * 1024, **more)


def gather(tokens, w_t, w_s):
    count = lax.axis_size("frame")
    each, patches, width = tokens.shape
    columns = w_t.shape[0]
    frames, lanes = count * each, 2 * patches
    f32, bf16 = jnp.float32, jnp.bfloat16
    shape = jax.ShapeDtypeStruct
    return pl.pallas_call(
        functools.partial(gather_kernel, count),
        out_shape=[
            shape((frames, patches, width), bf16),
            shape((frames, 1, width), f32),
            shape((frames // 2, columns, lanes), bf16),
            shape((frames, columns, lanes), bf16),
        ],
        in_specs=vmem(3),
        out_specs=vmem(4),
        scratch_shapes=[
            pltpu.VMEM((count, each, patches, width), bf16),
            pltpu.SemaphoreType.DMA((count - 1,)),
            pltpu.SemaphoreType.DMA((count - 1,)),
        ],
        compiler_params=limits(collective_id=0, has_side_effects=True),
    )(tokens, w_t, w_s)


def share_sum(part, small):
    frames, crops = lax.axis_size("frame"), lax.axis_size("crop")
    shape = jax.ShapeDtypeStruct
    dma = pltpu.SemaphoreType.DMA
    return pl.pallas_call(
        functools.partial(share_sum_kernel, frames, crops),
        out_shape=[shape(part.shape, part.dtype), shape(small.shape, small.dtype)],
        in_specs=vmem(2),
        out_specs=vmem(2),
        scratch_shapes=[
            pltpu.VMEM((frames,) + part.shape, part.dtype),
            pltpu.VMEM((frames * crops,) + small.shape, small.dtype),
            dma((frames - 1,)),
            dma((frames - 1,)),
            dma((frames * crops - 1,)),
            dma((frames * crops - 1,)),
        ],
        compiler_params=pltpu.CompilerParams(collective_id=1, has_side_effects=True),
    )(part, small)


def share(part):
    frames = lax.axis_size("frame")
    return pl.pallas_call(
        functools.partial(share_kernel, frames),
        out_shape=jax.ShapeDtypeStruct((frames,) + part.shape, part.dtype),
        in_specs=vmem(1),
        out_specs=vmem(1)[0],
        scratch_shapes=[
            pltpu.VMEM((frames,) + part.shape, part.dtype),
            pltpu.SemaphoreType.DMA((frames - 1,)),
            pltpu.SemaphoreType.DMA((frames - 1,)),
        ],
        compiler_params=pltpu.CompilerParams(collective_id=2, has_side_effects=True),
    )(part)


def forward(maps, t_half, s_frames):
    pairs, columns, lanes = t_half.shape
    heads = columns // (3 * HEAD)
    clips, steps = maps.shape
    f32 = jnp.float32
    shape = jax.ShapeDtypeStruct
    return pl.pallas_call(
        forward_kernel,
        out_shape=[
            shape((heads * HEAD, lanes), f32),
            shape((clips // 2, heads * HEAD, lanes), f32),
            shape((clips // 2, steps, columns, lanes), f32),
            shape((clips // 2, heads, steps, steps, lanes), f32),
            shape((clips // 2, heads, steps, lanes), f32),
        ],
        in_specs=[pl.BlockSpec(memory_space=pltpu.SMEM)] + vmem(2),
        out_specs=vmem(5),
        scratch_shapes=[pltpu.VMEM((pairs, columns, lanes), f32)],
        compiler_params=limits(),
    )(maps, t_half, s_frames)


def backward(first, heads, maps, grads, s_qkv, s_weights, s_cols, normed):
    pairs, steps, _, lanes = s_qkv.shape
    columns = heads * 3 * HEAD
    width = normed.shape[-1]
    return pl.pallas_call(
        functools.partial(backward_kernel, first, heads),
        out_shape=jax.ShapeDtypeStruct((width, columns), jnp.float32),
        in_specs=[pl.BlockSpec(memory_space=pltpu.SMEM)] + vmem(5),
        out_specs=vmem(1)[0],
        scratch_shapes=[
            pltpu.VMEM((steps, columns, lanes), jnp.float32),
            pltpu.VMEM((columns, pairs * steps * lanes), jnp.bfloat16),
            pltpu.VMEM((width, pairs * steps * lanes), jnp.bfloat16),
        ],
        compiler_params=limits(),
    )(maps, grads, s_qkv, s_weights, s_cols, normed)


def unit(vector):
    return vector * lax.rsqrt(jnp.sum(vector * vector, axis=-1, keepdims=True) + 1e-06)


def local(
    global_clips,
    frame_map,
    teacher_qkv,
    teacher_out,
    teacher_bottle,
    student_qkv,
    student_out,
    student_bottle,
    prototypes,
    center,
):
    f32 = jnp.float32
    tokens = global_clips[0]
    maps = frame_map[0]
    normed, sums, t_half, s_frames = gather(tokens, teacher_qkv.T, student_qkv.T)
    frames_all, patches, width = normed.shape
    sums = sums[:, 0]
    clips, steps = maps.shape
    spread = lax.axis_size("crop") * lax.axis_size("dp")
    place = lax.axis_index("crop") * lax.axis_size("dp") + lax.axis_index("dp")
    teacher_count = frames_all * patches * lax.axis_size("crop")
    local_count = steps * patches

    t_wide, s_wide, s_qkv, s_weights, s_cols = forward(maps, t_half, s_frames)
    rows = t_wide.shape[0]
    t_heads = jnp.sum(t_wide, axis=1)
    s_heads = (
        jnp.sum(s_wide.reshape(clips // 2, rows, 2, patches), axis=3)
        .transpose(0, 2, 1)
        .reshape(clips, rows)
    ) / local_count

    t_out32 = teacher_out.astype(f32)
    s_out32 = student_out.astype(f32)
    s_bottle32 = student_bottle.astype(f32)
    protos = prototypes.astype(f32)
    own = jnp.sum(tokens, axis=(0, 1), dtype=f32)
    t_partial = (own + jnp.dot(t_heads, t_out32, precision=HIGH)) / teacher_count
    t_z = jnp.dot(t_partial, teacher_bottle.astype(f32), precision=HIGH)
    s_partial = jnp.dot(s_heads, s_out32, precision=HIGH)
    picks = jnp.sum(
        (maps[:, :, None] == jnp.arange(frames_all, dtype=jnp.int32)[None, None, :]).astype(f32),
        axis=1,
    )
    local_mean = jnp.dot(picks, sums, precision=HIGH) / local_count

    bottle = t_z.shape[0]
    summed, t_sum = share_sum(
        s_partial.reshape(-1, 128), jnp.pad(t_z.reshape(-1, 128), ((0, 8 - bottle // 128), (0, 0)))
    )
    s_pooled = local_mean + summed.reshape(clips, width)
    unit_t = unit(t_sum[: bottle // 128].reshape(-1))
    s_z = jnp.dot(s_pooled, s_bottle32, precision=HIGH)
    inverse = lax.rsqrt(jnp.sum(s_z * s_z, axis=-1, keepdims=True) + 1e-06)
    unit_s = s_z * inverse

    units = jnp.concatenate([unit_s, unit_t[None]], axis=0)
    raw = jnp.dot(units, protos, precision=HIGH)
    logits = jnp.concatenate([raw[:clips] / TAU_STUD, (raw[clips:] - center) / TAU_TEACH], axis=0)
    top = jnp.max(logits, axis=-1, keepdims=True)
    weights = jnp.exp(logits - top)
    total = jnp.sum(weights, axis=-1, keepdims=True)
    expect = lax.dot_general(weights, protos, NT, precision=HIGH)
    shares = share(
        jnp.pad(
            jnp.concatenate([expect, total, top], axis=1), ((0, 7 - clips), (0, 126))
        )
    )[:, : clips + 1, : bottle + 2]
    tops = shares[:, :, bottle + 1 :]
    factor = jnp.exp(tops - jnp.max(tops, axis=0, keepdims=True))
    merged = jnp.sum(shares[:, :, : bottle + 1] * factor, axis=0)
    expect = merged[:, :bottle] / merged[:, bottle:]

    all_clips = clips * lax.axis_size("crop")
    d_unit = (expect[:clips] - expect[clips:]) / (all_clips * TAU_STUD)
    d_z = (d_unit - unit_s * jnp.sum(unit_s * d_unit, axis=-1, keepdims=True)) * inverse
    d_pooled = lax.dot_general(d_z, s_bottle32, NT, precision=HIGH)
    d_heads = lax.dot_general(d_pooled, s_out32, NT, precision=HIGH) / local_count

    wide = jnp.broadcast_to(
        d_heads.reshape(clips // 2, 2, rows).transpose(0, 2, 1)[..., None],
        (clips // 2, rows, 2, patches),
    ).reshape(clips // 2, rows, 2 * patches)
    heads = rows // HEAD
    first = heads // 2
    shares_g = [
        lax.psum_scatter(
            backward(at, many, maps, wide, s_qkv, s_weights, s_cols, normed),
            ("crop", "dp"),
            scatter_dimension=0,
            tiled=True,
        )
        for at, many in ((0, first), (first, heads - first))
        if many
    ]
    g_qkv = jnp.concatenate(shares_g, axis=1)

    few = lax.all_gather(
        jnp.concatenate([s_heads, s_pooled, d_z], axis=1), ("crop", "dp"), axis=0, tiled=True
    )
    size = width // spread
    all_heads = few[:, :rows]
    all_pooled = lax.dynamic_slice_in_dim(few[:, rows : rows + width], place * size, size, axis=1)
    all_d_z = few[:, rows + width :]
    some_bottle = lax.dynamic_slice_in_dim(s_bottle32, place * size, size, axis=0)
    g_bottle = jnp.dot(all_pooled.T, all_d_z, precision=HIGH)
    d_some = lax.dot_general(all_d_z, some_bottle, NT, precision=HIGH)
    g_out = jnp.dot(all_heads.T, d_some, precision=HIGH)
    return g_qkv, g_out, g_bottle


def solution(mesh):
    return jax.shard_map(
        local,
        mesh=mesh,
        in_specs=(
            P("dp", "frame", "crop", None),
            P("dp", "crop", None),
            P(None, "frame"),
            P("frame", None),
            P(),
            P(None, "frame"),
            P("frame", None),
            P(),
            P(None, "frame"),
            P("frame"),
        ),
        out_specs=(P(("crop", "dp"), "frame"), P("frame", ("crop", "dp")), P(("crop", "dp"), None)),
        check_vma=False,
    )
```
